32 devices in a mesh: rep: 2 (over y), ada: 16 (over z, x, core).
Axes of the slice: x: 2, y: 2, z: 4, core: 2. Of those that a mesh axis runs over, the one named last changes fastest.
Arguments:
- activations: bfloat16 [4096, 8192], P(('rep', 'ada')), parts along dimension 0, may hold values from -1.5 to 1.5
- out_grads: bfloat16 [4096, 1024], P(('rep', 'ada')), parts along dimension 0, may hold values from -6 to 6
- base_weight: bfloat16 [8192, 1024], P('ada'), may hold values from -0.1875 to 0.1875
- adapter_in: bfloat16 [32, 8192, 128], P(('rep', 'ada')), parts along dimension 0, may hold values from -0.125 to 0.125
- adapter_out: bfloat16 [32, 128, 1024], P(('rep', 'ada')), parts along dimension 0, may hold values from -0.1875 to 0.1875
- tenant_ids: int32 [4096], P(('rep', 'ada')), parts along dimension 0, may hold values from 0 to 15, as said below
- slot_of: int32 [32], P('rep'), parts along dimension 0, may hold values from 0 to 15, each once
- ranks: int32 [32], P('rep'), parts along dimension 0, may hold values from 16 to 128, as said below
Outputs:
- input_grads: bfloat16 [4096, 8192], P(('rep', 'ada')), parts along dimension 0
- grad_in: float32 [32, 8192, 128], P(('rep', 'ada')), parts along dimension 0
- grad_out: float32 [32, 128, 1024], P(('rep', 'ada')), parts along dimension 0
The draws below stay inside these ranges and needn't reach their ends.
There are 2 independent parts, one for each index of `rep`. The reference program is written for one: setup_inputs(seed, part) draws one part's arguments, and reference() takes and returns one part's arrays. A program takes and returns all parts, laid end to end along the dimension named above; an argument that names none is the same for every part. Nothing has to cross between parts.
Inputs may be any that keep to these rules, and one draw needn't show every extreme that they name: `tenant_ids`: the 128 tokens of one device name one tenant at most 16 times; in every draw one tenant is named exactly 16 times by the tokens of every device. `slot_of`: each slot holds exactly one tenant. `ranks`: multiples of 16.
All inputs are finite; a program needn't handle non-finite values.
Results may differ from the reference program's by a relative error of at most 0.0034.
Values may be sent and summed in bfloat16 or wider, within the bound.
A program may use at most 128 MiB of HBM per device.

```python
import jax
import jax.numpy as jnp
from jax import lax

D = 8192
DK = 1024
RMAX = 128
TOK_DEV = 128
TENANTS = 16
CAP = 16
TOKENS = 2048
N_ADA = 16


def draw_tenant_ids(key, part):
    key = jax.random.fold_in(key, 11)
    blocks = TOKENS // TOK_DEV
    pool = TENANTS * CAP
    relabel = jax.random.permutation(jax.random.fold_in(key, 1), TENANTS).astype(jnp.int32)

    def one_block(block_key):
        first_key, second_key = jax.random.split(block_key)
        shuffled = jax.random.permutation(first_key, pool - CAP) + CAP
        labels = jnp.concatenate([jnp.zeros((CAP,), jnp.int32), (shuffled[:TOK_DEV - CAP] // CAP).astype(jnp.int32)])
        return jax.random.permutation(second_key, labels)
    block_keys = jax.random.split(jax.random.fold_in(key, 2), blocks)
    labels = jax.vmap(one_block)(block_keys).reshape(-1)
    return relabel[labels].astype(jnp.int32)


def draw_ranks(key, part):
    key = jax.random.fold_in(key, 12)
    first_key, second_key = jax.random.split(key)
    step_size = RMAX // 8
    values = step_size * (1 + jax.random.randint(first_key, (TENANTS,), 0, 8))
    chosen = jax.random.randint(second_key, (), 0, TENANTS)
    places = jnp.arange(TENANTS)
    values = jnp.where(places == chosen, RMAX, values)
    values = jnp.where(places == (chosen + 1) % TENANTS, step_size, values)
    return values.astype(jnp.int32)


def levels(rng, shape, cuts, smallest, largest):
    gain = 1.0
    for axis_at, shards_of in cuts:
        draws = jax.random.uniform(jax.random.fold_in(jax.random.fold_in(rng, 6), axis_at), (shards_of,), jnp.float32, smallest / len(cuts), largest / len(cuts))
        gain = gain * jnp.repeat(jnp.exp(draws), shape[axis_at] // shards_of).reshape((-1,) + (1,) * (len(shape) - 1 - axis_at))
    return gain


def normal_values(rng, shape, spread, most, pieces=(), kind=jnp.bfloat16):
    loudness = levels(rng, shape, pieces, -0.22, 0.18) if pieces else 1.0
    drawn = jax.random.normal(rng, shape, jnp.float32) * spread * loudness
    return jnp.minimum(jnp.maximum(drawn, -most), most).astype(kind)


def setup_inputs(seed: int = 0, part: int = 0) -> dict:
    key_list = jax.random.split(jax.random.key(seed), 9)
    own_keys = jax.random.split(jax.random.fold_in(key_list[8], part), 9)
    activations = normal_values(own_keys[0], (TOKENS, D), 0.25, 1.5, ((0, 16),))
    out_grads = normal_values(own_keys[1], (TOKENS, DK), 1.0, 6.0, ((0, 16),))
    base_weight = normal_values(key_list[2], (D, DK), DK ** -0.5, 0.1875, ((0, 16),))
    adapter_in = normal_values(own_keys[3], (TENANTS, D, RMAX), (D // 4) ** -0.5, 0.125, ((0, 16),))
    adapter_out = normal_values(own_keys[4], (TENANTS, RMAX, DK), DK ** -0.5, 0.1875, ((0, 16),))
    tenant_ids = draw_tenant_ids(jax.random.fold_in(jax.random.fold_in(key_list[8], part), 71), part)
    slot_of = jax.random.permutation(own_keys[6], TENANTS).astype(jnp.int32)
    ranks = draw_ranks(jax.random.fold_in(jax.random.fold_in(key_list[8], part), 71), part)
    return dict(activations=activations, out_grads=out_grads, base_weight=base_weight, adapter_in=adapter_in, adapter_out=adapter_out, tenant_ids=tenant_ids, slot_of=slot_of, ranks=ranks)


def reference(activations, out_grads, base_weight, adapter_in, adapter_out, tenant_ids, slot_of, ranks):
    width = N_ADA * CAP
    tenant_range = jnp.arange(TENANTS, dtype=jnp.int32)
    token_slot = lax.optimization_barrier(jnp.sum(jnp.where(tenant_ids[:, None] == tenant_range[None, :], slot_of[None, :], 0), axis=1)).astype(jnp.int32)
    order = jnp.argsort(token_slot, stable=True).astype(jnp.int32)
    inverse = jnp.argsort(order).astype(jnp.int32)
    counts = lax.optimization_barrier(jnp.sum((token_slot[None, :] == tenant_range[:, None]).astype(jnp.int32), axis=1)).astype(jnp.int32)
    starts = (jnp.cumsum(counts) - counts).astype(jnp.int32)
    sorted_x = jnp.concatenate([activations[order], jnp.zeros((width, D), activations.dtype)], axis=0)
    sorted_g = jnp.concatenate([out_grads[order], jnp.zeros((width, DK), out_grads.dtype)], axis=0)
    rank_of_slot = jnp.zeros((TENANTS,), jnp.int32).at[slot_of].set(ranks)
    columns = jnp.arange(RMAX, dtype=jnp.int32)

    def per_slot(slot):
        begin = starts[slot]
        live = jnp.arange(width, dtype=jnp.int32) < counts[slot]
        block_x = lax.dynamic_slice_in_dim(sorted_x, begin, width, 0)
        block_g = lax.dynamic_slice_in_dim(sorted_g, begin, width, 0)
        block_x = jnp.where(live[:, None], block_x, jnp.zeros_like(block_x))
        block_g = jnp.where(live[:, None], block_g, jnp.zeros_like(block_g))
        own_rank = rank_of_slot[slot]
        keep = columns < own_rank
        scale = 4.0 / jnp.sqrt(own_rank.astype(jnp.float32))
        down = jnp.where(keep[None, :], adapter_in[slot], jnp.zeros_like(adapter_in[slot]))
        upper = jnp.where(keep[:, None], adapter_out[slot], jnp.zeros_like(adapter_out[slot]))
        projected = jnp.dot(block_x, down, preferred_element_type=jnp.float32).astype(jnp.bfloat16)
        inner_grad = (scale * jnp.dot(block_g, upper.T, preferred_element_type=jnp.float32)).astype(jnp.bfloat16)
        grad_out = scale * jnp.dot(projected.T, block_g, preferred_element_type=jnp.float32)
        grad_in = jnp.dot(block_x.T, inner_grad, preferred_element_type=jnp.float32)
        returned = jnp.dot(inner_grad, down.T, preferred_element_type=jnp.float32).astype(jnp.bfloat16)
        return (grad_in, grad_out, returned)
    grad_in, grad_out, returned = lax.map(per_slot, tenant_range)
    sorted_slot = token_slot[order]
    within = jnp.arange(TOKENS, dtype=jnp.int32) - starts[sorted_slot]
    flat_index = (sorted_slot * width + within).astype(jnp.int32)
    adapter_sorted = returned.reshape(TENANTS * width, D)[flat_index]
    adapter_term = adapter_sorted[inverse]
    base = jnp.dot(out_grads, base_weight.T, preferred_element_type=jnp.float32)
    input_grads = (base + adapter_term.astype(jnp.float32)).astype(jnp.bfloat16)
    return (input_grads, grad_in, grad_out)
```

```python
import functools

import jax
import jax.numpy as jnp
from jax import lax
from jax.experimental import pallas as pl
from jax.experimental.pallas import tpu as pltpu
from jax.sharding import PartitionSpec as P

MESH = pl.DeviceIdType.MESH
NT = (((1,), (1,)), ((), ()))
TN = (((0,), (0,)), ((), ()))
LANES = 128
F32 = jnp.float32
BF16 = jnp.bfloat16


def dot_f32(a, b, dims):
    return lax.dot_general(a, b, dims, preferred_element_type=F32)


def kernel(
    n, parts,
    x_ref, gb_ref, w_ref, a_ref, place_ref, cmask_ref, own_ref,
    out_ref, gin_ref, gout_ref,
    gball, pall, acat, xsel, xrecv, ret, inner, tslot, rg, gin, gout,
    g_recv, g_send, p_recv, p_send, a_recv, a_send, x_recv, x_send, r_recv, r_send,
    local_sem, gin_sem, gout_sem, ownret_sem,
):
    me = lax.axis_index("ada")
    z, lane = me // 4, me % 4
    xx, core = lane // 2, lane % 2
    nz = n // 4
    rows = gb_ref.shape[1]
    dim = x_ref.shape[1]
    cols = dim // n
    width = dim // parts
    cap = xsel.shape[1] // n
    step = 512

    def index(zo, xo, co):
        return zo * 4 + xo * 2 + co

    def remote(src, dst, send, recv, target):
        return pltpu.make_async_remote_copy(
            src_ref=src, dst_ref=dst, send_sem=send, recv_sem=recv,
            device_id={"ada": target}, device_id_type=MESH,
        )

    barrier = pltpu.get_barrier_semaphore()
    for k in range(1, n):
        pl.semaphore_signal(
            barrier, inc=1, device_id={"ada": (me + k) % n}, device_id_type=MESH
        )
    pl.semaphore_wait(barrier, n - 1)

    def block(o):
        return gball.at[:, pl.ds(pl.multiple_of(o * rows, rows), rows), :]

    def gcopy(kind, o, target, first=False):
        return remote(
            gb_ref if first else block(o), block(o), g_send.at[kind, o], g_recv.at[o], target
        )

    def wait_g(o):
        gcopy(0, o, (me + 1) % n).wait_recv()

    other_x = index(z, 1 - xx, core)
    other_core = index(z, xx, 1 - core)
    above = (me + 4) % n
    below = (me + n - 4) % n

    def z_up(o, first=False):
        @pl.when(z < nz - 1)
        def _():
            gcopy(0, o, above, first).start()

    def z_down(o, first=False):
        @pl.when(z > 0)
        def _():
            gcopy(1, o, below, first).start()

    z_up(me, True)
    z_down(me, True)
    gcopy(2, me, other_x, True).start()
    gcopy(3, me, other_core, True).start()
    own_gb = pltpu.make_async_copy(gb_ref, block(me), local_sem.at[0])
    own_gb.start()

    def pcopy(k):
        target = (me + k) % n
        return remote(place_ref, pall.at[me], p_send.at[k], p_recv.at[me], target)

    for k in range(1, n):
        pcopy(k).start()
    own_p = pltpu.make_async_copy(place_ref, pall.at[me], local_sem.at[1])
    own_p.start()

    def acopy(k):
        target = (me + k) % n
        return remote(
            a_ref.at[pl.ds(pl.multiple_of(target * cols, cols), cols), :],
            acat.at[:, pl.ds(pl.multiple_of(me * LANES, LANES), LANES)],
            a_send.at[k], a_recv.at[me], target,
        )

    for k in range(1, n):
        acopy(k).start()
    own_a = pltpu.make_async_copy(
        a_ref.at[pl.ds(pl.multiple_of(me * cols, cols), cols), :],
        acat.at[:, pl.ds(pl.multiple_of(me * LANES, LANES), LANES)],
        local_sem.at[2],
    )
    own_a.start()

    placed = place_ref[1:2, :]
    pick = (
        lax.broadcasted_iota(jnp.int32, (n * cap, rows), 0) == placed
    ).astype(F32).astype(BF16)
    for q in range(parts):
        @pl.loop(0, width // step)
        def _(i):
            to = pl.ds(pl.multiple_of(i * step, step), step)
            at = pl.ds(pl.multiple_of(q * width + i * step, step), step)
            xsel[q, :, to] = jnp.dot(
                pick, x_ref[:, at], preferred_element_type=F32
            ).astype(BF16)

    own_gb.wait()
    for k in range(1, nz):
        @pl.when(z - k >= 0)
        def _():
            o = me - 4 * k
            wait_g(o)
            z_up(o)
            gcopy(2, o, other_x).start()
            gcopy(3, o, other_core).start()

        @pl.when(z + k < nz)
        def _():
            o = me + 4 * k
            wait_g(o)
            z_down(o)
            gcopy(2, o, other_x).start()
            gcopy(3, o, other_core).start()
    for zo in range(nz):
        o = index((z + zo) % nz, 1 - xx, core)
        wait_g(o)
        gcopy(3, o, other_core).start()

    def xcopy(q, k):
        target = (me + k) % n
        return remote(
            xsel.at[q, pl.ds(pl.multiple_of(target * cap, cap), cap), :],
            xrecv.at[q, pl.ds(pl.multiple_of(me * cap, cap), cap), :],
            x_send.at[q, k], x_recv.at[q, me], target,
        )

    own_x = []
    for q in range(parts):
        for k in range(1, n):
            xcopy(q, k).start()
        own_x.append(pltpu.make_async_copy(
            xsel.at[q, pl.ds(pl.multiple_of(me * cap, cap), cap), :],
            xrecv.at[q, pl.ds(pl.multiple_of(me * cap, cap), cap), :],
            local_sem.at[4 + q],
        ))
        own_x[-1].start()

    for zo in range(nz):
        for xo in range(2):
            wait_g(index((z + zo) % nz, xo, 1 - core))
    own_p.wait()
    for k in range(1, n):
        o = (me + k) % n
        remote(place_ref, pall.at[o], p_send.at[k], p_recv.at[o], o).wait_recv()

    @pl.loop(0, n)
    def _(d):
        at = pl.ds(pl.multiple_of(d * rows, rows), rows)
        tslot[at, :] = jnp.broadcast_to(pall[d, 0:1, :], (rows, LANES)).T
        mine = (
            lax.broadcasted_iota(jnp.int32, (cap, rows), 0) + me * cap == pall[d, 1:2, :]
        ).astype(F32).astype(BF16)
        rg[pl.ds(pl.multiple_of(d * cap, cap), cap), :] = jnp.dot(
            mine, gball[0, at, :], preferred_element_type=F32
        ).astype(BF16)

    scaled_keep, keep, scale = own_ref[0:1, :], own_ref[1:2, :], own_ref[2:3, 0:1]
    ig = (scaled_keep * dot_f32(rg[...], gb_ref[1], NT)).astype(BF16)

    own_a.wait()
    for k in range(1, n):
        o = (me + k) % n
        remote(
            a_ref.at[pl.ds(0, cols), :],
            acat.at[:, pl.ds(pl.multiple_of(o * LANES, LANES), LANES)],
            a_send.at[k], a_recv.at[o], o,
        ).wait_recv()

    quad = 4 * rows
    slots_step = step // LANES

    def rcopy(target):
        return remote(
            ret.at[pl.ds(pl.multiple_of(target * rows, rows), rows), :],
            out_ref.at[:, pl.ds(pl.multiple_of(me * cols, cols), cols)],
            r_send.at[target], r_recv.at[me], target,
        )

    own_ret = pltpu.make_async_copy(
        ret.at[pl.ds(pl.multiple_of(me * rows, rows), rows), :],
        out_ref.at[:, pl.ds(pl.multiple_of(me * cols, cols), cols)],
        ownret_sem,
    )

    @pl.loop(0, nz)
    def _(i):
        zt = (z + 1 + i) % nz
        at = pl.ds(pl.multiple_of(zt * quad, quad), quad)

        @pl.loop(0, n * LANES // step)
        def _(j):
            to = pl.ds(pl.multiple_of(j * step, step), step)
            acc = dot_f32(gball[0, at, :], gball[1, to, :], NT) * cmask_ref[0:1, to]
            for s in range(slots_step):
                hit = tslot[at, :] == j * slots_step + s
                part = pl.ds(pl.multiple_of(j * step + s * LANES, LANES), LANES)
                inner[:, part] = jnp.where(
                    hit, acc[:, s * LANES:(s + 1) * LANES], 0.0
                ).astype(BF16)

        term = dot_f32(inner[...], acat[...], NT).astype(BF16).astype(F32)
        ret[at, :] = (dot_f32(gball[0, at, :], w_ref[...], NT) + term).astype(BF16)
        for t in range(4):
            target = zt * 4 + t

            @pl.when(target != me)
            def _():
                rcopy(target).start()

            @pl.when(target == me)
            def _():
                own_ret.start()

    proj = jnp.zeros((n * cap, LANES), F32)
    for q in range(parts):
        own_x[q].wait()
        for k in range(1, n):
            o = (me + k) % n
            remote(
                xsel.at[q, pl.ds(0, cap), :],
                xrecv.at[q, pl.ds(pl.multiple_of(o * cap, cap), cap), :],
                x_send.at[q, k], x_recv.at[q, o], o,
            ).wait_recv()
        proj += jnp.dot(
            xrecv[q], a_ref[pl.ds(q * width, width), :], preferred_element_type=F32
        )

        @pl.loop(0, width // step)
        def _(i):
            at = pl.ds(pl.multiple_of(i * step, step), step)
            gin[q, at, :] = dot_f32(xrecv[q, :, at], ig, TN)

        pltpu.make_async_copy(
            gin.at[q], gin_ref.at[pl.ds(q * width, width), :], gin_sem.at[q]
        ).start()
    projected = (proj * keep).astype(BF16)
    gout[...] = scale * dot_f32(projected, rg[...], TN)
    out_copy = pltpu.make_async_copy(gout, gout_ref, gout_sem)
    out_copy.start()

    own_ret.wait()
    for k in range(1, n):
        o = (me + k) % n
        remote(
            ret.at[pl.ds(0, rows), :],
            out_ref.at[:, pl.ds(pl.multiple_of(o * cols, cols), cols)],
            r_send.at[o], r_recv.at[o], o,
        ).wait_recv()
        rcopy(o).wait_send()
        acopy(k).wait_send()
        pcopy(k).wait_send()
        for q in range(parts):
            xcopy(q, k).wait_send()
    for zo in range(nz):
        o = index(zo, xx, core)
        gcopy(2, o, other_x).wait_send()
        gcopy(3, o, other_core).wait_send()
        gcopy(3, index(zo, 1 - xx, core), other_core).wait_send()

        @pl.when((zo <= z) & (z < nz - 1))
        def _():
            gcopy(0, o, above).wait_send()

        @pl.when((zo >= z) & (z > 0))
        def _():
            gcopy(1, o, below).wait_send()
    for q in range(parts):
        pltpu.make_async_copy(
            gin.at[q], gin_ref.at[pl.ds(q * width, width), :], gin_sem.at[q]
        ).wait()
    out_copy.wait()


def routed(activations, out_grads, base_weight, adapter_in, adapter_out, tenant_ids, slot_of, ranks):
    n = lax.axis_size("ada")
    rows, dim = activations.shape
    dk = out_grads.shape[1]
    cap = max(2, 2 * rows // n)
    cols = dim // n
    parts = 4
    tenants = jnp.arange(slot_of.shape[0], dtype=jnp.int32)
    destination = jnp.sum(
        jnp.where(tenant_ids[:, None] == tenants[None, :], slot_of[None, :], 0), axis=1
    )
    onehot = (destination[:, None] == tenants[None, :]).astype(jnp.int32)
    earlier = jnp.arange(rows)[:, None] > jnp.arange(rows)[None, :]
    same = destination[:, None] == destination[None, :]
    position = jnp.sum((earlier & same).astype(jnp.int32), axis=1)
    placed = destination * cap + position
    place = jnp.zeros((8, rows), jnp.int32).at[0].set(destination).at[1].set(placed)
    slot_rank = jnp.sum(jnp.where(slot_of[None, :] == tenants[:, None], ranks[None, :], 0), axis=1)
    scale = 4.0 / jnp.sqrt(slot_rank.astype(F32))
    keep = (jnp.arange(LANES, dtype=jnp.int32)[None, :] < slot_rank[:, None]).astype(F32)
    cmask = (scale[:, None] * keep).reshape(1, -1)
    mine = tenants == lax.axis_index("ada")
    own_scale = jnp.sum(jnp.where(mine, scale, 0.0))
    own_keep = jnp.sum(jnp.where(mine[:, None], keep, 0.0), axis=0)
    own = jnp.stack([own_scale * own_keep, own_keep, jnp.full((LANES,), own_scale)])
    own = jnp.pad(own, ((0, 5), (0, 0)))
    gb = jnp.stack([out_grads, adapter_out[0]])
    vmem = pl.BlockSpec(memory_space=pltpu.VMEM)
    any_space = pl.BlockSpec(memory_space=pl.ANY)
    dma = pltpu.SemaphoreType.DMA
    input_grads, grad_in, grad_out = pl.pallas_call(
        functools.partial(kernel, n, parts),
        out_shape=(
            jax.ShapeDtypeStruct((rows, dim), BF16),
            jax.ShapeDtypeStruct((dim, LANES), F32),
            jax.ShapeDtypeStruct((LANES, dk), F32),
        ),
        in_specs=[vmem] * 7,
        out_specs=(any_space,) * 3,
        scratch_shapes=[
            pltpu.VMEM((2, n * rows, dk), BF16),
            pltpu.VMEM((n, 8, rows), jnp.int32),
            pltpu.VMEM((cols, n * LANES), BF16),
            pltpu.VMEM((parts, n * cap, dim // parts), BF16),
            pltpu.VMEM((parts, n * cap, dim // parts), BF16),
            pltpu.VMEM((n * rows, cols), BF16),
            pltpu.VMEM((4 * rows, n * LANES), BF16),
            pltpu.VMEM((n * rows, LANES), jnp.int32),
            pltpu.VMEM((n * cap, dk), BF16),
            pltpu.VMEM((parts, dim // parts, LANES), F32),
            pltpu.VMEM((LANES, dk), F32),
            dma((n,)), dma((4, n)),
            dma((n,)), dma((n,)),
            dma((n,)), dma((n,)),
            dma((parts, n)), dma((parts, n)),
            dma((n,)), dma((n,)),
            dma((4 + parts,)), dma((parts,)), dma, dma,
        ],
        compiler_params=pltpu.CompilerParams(
            collective_id=0, has_side_effects=True, vmem_limit_bytes=56 * 2**20
        ),
        cost_estimate=pl.CostEstimate(
            flops=17 * 10**9, bytes_accessed=12 * 2**20, transcendentals=0
        ),
    )(activations, gb, base_weight, adapter_in[0], place, cmask, own)
    return (input_grads, grad_in[None], grad_out[None])


def base_term(out_grads, base_weight):
    return lax.dot_general(
        out_grads,
        lax.all_gather(base_weight, "ada", axis=0, tiled=True),
        (((1,), (1,)), ((), ())),
        preferred_element_type=jnp.float32,
    )


def adapter_part(activations, out_grads, adapter_in, adapter_out, tenant_ids, slot_of, ranks):
    peers = lax.axis_size("ada")
    local_rows = activations.shape[0]
    capacity = max(2, 2 * local_rows // peers)
    tenant_count = slot_of.shape[0]
    tenant_range = jnp.arange(tenant_count, dtype=jnp.int32)
    destination = jnp.sum(
        jnp.where(tenant_ids[:, None] == tenant_range[None, :], slot_of[None, :], 0), axis=1
    )
    onehot = (destination[:, None] == jnp.arange(peers, dtype=jnp.int32)[None, :]).astype(jnp.int32)
    running = jnp.cumsum(onehot, axis=0)
    position = jnp.sum(onehot * running, axis=1) - 1
    placed = destination * capacity + position
    selector = (placed[None, :] == jnp.arange(peers * capacity, dtype=jnp.int32)[:, None]).astype(
        jnp.bfloat16
    )
    send_x = jnp.dot(selector, activations, preferred_element_type=jnp.float32).astype(jnp.bfloat16)
    send_g = jnp.dot(selector, out_grads, preferred_element_type=jnp.float32).astype(jnp.bfloat16)
    recv_x, recv_g = (
        lax.all_to_all(send_x, "ada", split_axis=0, concat_axis=0, tiled=True),
        lax.all_to_all(send_g, "ada", split_axis=0, concat_axis=0, tiled=True),
    )
    owner_index = lax.axis_index("ada")
    own_rank = jnp.sum(jnp.where(slot_of == owner_index, ranks, 0))
    scale = 4.0 / jnp.sqrt(own_rank.astype(jnp.float32))
    keep = jnp.arange(adapter_in.shape[2], dtype=jnp.int32) < own_rank
    down = jnp.where(keep[None, :], adapter_in[0], jnp.zeros_like(adapter_in[0]))
    upper = jnp.where(keep[:, None], adapter_out[0], jnp.zeros_like(adapter_out[0]))
    projected = jnp.dot(recv_x, down, preferred_element_type=jnp.float32).astype(jnp.bfloat16)
    inner_grad = (
        scale
        * lax.dot_general(
            recv_g, upper, (((1,), (1,)), ((), ())), preferred_element_type=jnp.float32
        )
    ).astype(jnp.bfloat16)
    grad_out = scale * lax.dot_general(
        projected, recv_g, (((0,), (0,)), ((), ())), preferred_element_type=jnp.float32
    )
    grad_in = lax.dot_general(
        recv_x, inner_grad, (((0,), (0,)), ((), ())), preferred_element_type=jnp.float32
    )
    returned = lax.dot_general(
        inner_grad, down, (((1,), (1,)), ((), ())), preferred_element_type=jnp.float32
    ).astype(jnp.bfloat16)
    arrived = lax.all_to_all(returned, "ada", split_axis=0, concat_axis=0, tiled=True)
    adapter_term = lax.dot_general(
        selector, arrived, (((0,), (0,)), ((), ())), preferred_element_type=jnp.float32
    )
    return (adapter_term, grad_in[None], grad_out[None])


def gathered(
    activations, out_grads, base_weight, adapter_in, adapter_out, tenant_ids, slot_of, ranks
):
    base = base_term(out_grads, base_weight)
    adapter_term, grad_in, grad_out = adapter_part(
        activations, out_grads, adapter_in, adapter_out, tenant_ids, slot_of, ranks
    )
    input_grads = (base + adapter_term).astype(jnp.bfloat16)
    return (input_grads, grad_in, grad_out)


def shards(activations, *rest):
    n = lax.axis_size("ada")
    rows, dim = activations.shape
    whole = n % 4 == 0 and rows == LANES and (2 * rows // n) % 16 == 0 and dim % (512 * n) == 0
    return (routed if whole else gathered)(activations, *rest)


def solution(mesh):
    placed = (
        P(("rep", "ada"), None),
        P(("rep", "ada"), None),
        P("ada", None),
        P(("rep", "ada"), None, None),
        P(("rep", "ada"), None, None),
        P(("rep", "ada")),
        P("rep"),
        P("rep"),
    )
    return jax.shard_map(
        shards,
        mesh=mesh,
        in_specs=placed,
        out_specs=(
            P(("rep", "ada"), None),
            P(("rep", "ada"), None, None),
            P(("rep", "ada"), None, None),
        ),
        check_vma=False,
    )
```

```python
import functools

import jax
import jax.numpy as jnp
from jax import lax
from jax.experimental import pallas as pl
from jax.experimental.pallas import tpu as pltpu
from jax.sharding import PartitionSpec as P

MESH = pl.DeviceIdType.MESH
NT = (((1,), (1,)), ((), ()))
TN = (((0,), (0,)), ((), ()))
LANES = 128
F32 = jnp.float32
BF16 = jnp.bfloat16


def dot_f32(a, b, dims):
    return lax.dot_general(a, b, dims, preferred_element_type=F32)


def kernel(
    n, parts, early,
    x_ref, g_ref, b_ref, w_ref, a_ref, place_ref, own_ref,
    out_ref, gin_ref, gout_ref,
    gall, iall, pall, acat, xsel, xrecv, ret, back, ig, rg, gin, gout,
    g_recv, g_send, i_recv, i_send, p_recv, p_send, a_recv, a_send, x_recv, x_send, r_recv, r_send,
    local_sem, gin_sem, gout_sem, ownret_sem,
):
    me = lax.axis_index("ada")
    z, lane = me // 4, me % 4
    xx, core = lane // 2, lane % 2
    nz = n // 4
    rows = g_ref.shape[0]
    dim = x_ref.shape[1]
    cols = dim // n
    width = dim // parts
    cap = xsel.shape[1] // n
    step = 512

    def index(zo, xo, co):
        return zo * 4 + xo * 2 + co

    def remote(src, dst, send, recv, target):
        return pltpu.make_async_remote_copy(
            src_ref=src, dst_ref=dst, send_sem=send, recv_sem=recv,
            device_id={"ada": target}, device_id_type=MESH,
        )

    barrier = pltpu.get_barrier_semaphore()
    for k in range(1, n):
        pl.semaphore_signal(
            barrier, inc=1, device_id={"ada": (me + k) % n}, device_id_type=MESH
        )
    pl.semaphore_wait(barrier, n - 1)

    other_x = index(z, 1 - xx, core)
    other_core = index(z, xx, 1 - core)
    above = (me + 4) % n
    below = (me + n - 4) % n

    def gather(own_ref, block, send_sem, recv_sem):
        def copy(kind, o, target, first=False):
            return remote(
                own_ref if first else block(o), block(o), send_sem.at[kind, o], recv_sem.at[o],
                target,
            )

        def wait(o):
            copy(0, o, above).wait_recv()

        def pass_on(o, first=False):
            copy(2, o, other_x, first).start()
            copy(3, o, other_core, first).start()

        def up(o, first=False):
            @pl.when(z < nz - 1)
            def _():
                copy(0, o, above, first).start()

        def down(o, first=False):
            @pl.when(z > 0)
            def _():
                copy(1, o, below, first).start()

        def begin():
            up(me, True)
            down(me, True)
            pass_on(me, True)

        def relay(fill):
            for k in range(1, nz):
                @pl.when(z - k >= 0)
                def _():
                    wait(me - 4 * k)
                    up(me - 4 * k)
                    pass_on(me - 4 * k)

                @pl.when(z + k < nz)
                def _():
                    wait(me + 4 * k)
                    down(me + 4 * k)
                    pass_on(me + 4 * k)

                fill()
            for zo in range(nz):
                o = index((z + zo) % nz, 1 - xx, core)
                wait(o)
                copy(3, o, other_core).start()
            fill()

        def finish():
            for zo in range(nz):
                for xo in range(2):
                    wait(index((z + zo) % nz, xo, 1 - core))

        def drain():
            for zo in range(nz):
                o = index(zo, xx, core)
                copy(2, o, other_x).wait_send()
                copy(3, o, other_core).wait_send()
                copy(3, index(zo, 1 - xx, core), other_core).wait_send()

                @pl.when((zo <= z) & (z < nz - 1))
                def _():
                    copy(0, o, above).wait_send()

                @pl.when((zo >= z) & (z > 0))
                def _():
                    copy(1, o, below).wait_send()

        return begin, relay, finish, drain

    def g_block(o):
        return gall.at[pl.ds(pl.multiple_of(o * rows, rows), rows), :]

    g_begin, g_relay, g_finish, g_drain = gather(g_ref, g_block, g_send, g_recv)
    i_begin, i_relay, i_finish, i_drain = gather(ig, lambda o: iall.at[o], i_send, i_recv)
    g_begin()
    own_g = pltpu.make_async_copy(g_ref, g_block(me), local_sem.at[0])
    own_g.start()

    def pcopy(k):
        target = (me + k) % n
        return remote(place_ref, pall.at[me], p_send.at[k], p_recv.at[me], target)

    for k in range(1, n):
        pcopy(k).start()
    own_p = pltpu.make_async_copy(place_ref, pall.at[me], local_sem.at[1])
    own_p.start()

    def acopy(k):
        target = (me + k) % n
        return remote(
            a_ref.at[pl.ds(pl.multiple_of(target * cols, cols), cols), :],
            acat.at[:, pl.ds(pl.multiple_of(me * LANES, LANES), LANES)],
            a_send.at[k], a_recv.at[me], target,
        )

    a_left = list(range(1, n))

    def some_a():
        for _ in range(min(len(a_left), n)):
            acopy(a_left.pop(0)).start()

    some_a()
    own_a = pltpu.make_async_copy(
        a_ref.at[pl.ds(pl.multiple_of(me * cols, cols), cols), :],
        acat.at[:, pl.ds(pl.multiple_of(me * LANES, LANES), LANES)],
        local_sem.at[2],
    )
    own_a.start()

    placed = place_ref[1:2, :]
    pick = (
        lax.broadcasted_iota(jnp.int32, (n * cap, rows), 0) == placed
    ).astype(F32).astype(BF16)
    for q in range(parts):
        @pl.loop(0, width // step)
        def _(i):
            to = pl.ds(pl.multiple_of(i * step, step), step)
            at = pl.ds(pl.multiple_of(q * width + i * step, step), step)
            xsel[q, :, to] = jnp.dot(
                pick, x_ref[:, at], preferred_element_type=F32
            ).astype(BF16)

    own_g.wait()
    g_relay(some_a)
    while a_left:
        some_a()

    def xcopy(q, k):
        target = (me + k) % n
        return remote(
            xsel.at[q, pl.ds(pl.multiple_of(target * cap, cap), cap), :],
            xrecv.at[q, pl.ds(pl.multiple_of(me * cap, cap), cap), :],
            x_send.at[q, k], x_recv.at[q, me], target,
        )

    own_x = []

    def send_x(q):
        for k in range(1, n):
            xcopy(q, k).start()
        own_x.append(pltpu.make_async_copy(
            xsel.at[q, pl.ds(pl.multiple_of(me * cap, cap), cap), :],
            xrecv.at[q, pl.ds(pl.multiple_of(me * cap, cap), cap), :],
            local_sem.at[4 + q],
        ))
        own_x[-1].start()

    x_left = list(range(parts))

    def some_x():
        if x_left:
            send_x(x_left.pop(0))

    for _ in range(early):
        some_x()
    g_finish()
    own_p.wait()
    for k in range(1, n):
        o = (me + k) % n
        remote(place_ref, pall.at[o], p_send.at[k], p_recv.at[o], o).wait_recv()

    @pl.loop(0, n)
    def _(d):
        mine = (
            lax.broadcasted_iota(jnp.int32, (cap, rows), 0) + me * cap == pall[d, 1:2, :]
        ).astype(F32).astype(BF16)
        rg[pl.ds(pl.multiple_of(d * cap, cap), cap), :] = jnp.dot(
            mine, gall[pl.ds(pl.multiple_of(d * rows, rows), rows), :],
            preferred_element_type=F32,
        ).astype(BF16)

    scaled_keep, keep, scale = own_ref[0:1, :], own_ref[1:2, :], own_ref[2:3, 0:1]
    ig[...] = (scaled_keep * dot_f32(rg[...], b_ref[...], NT)).astype(BF16)
    i_begin()
    own_i = pltpu.make_async_copy(ig, iall.at[me], local_sem.at[3])
    own_i.start()
    own_i.wait()
    some_x()
    i_relay(some_x)
    while x_left:
        some_x()
    i_finish()

    own_a.wait()
    for k in range(1, n):
        o = (me + k) % n
        remote(
            a_ref.at[pl.ds(0, cols), :],
            acat.at[:, pl.ds(pl.multiple_of(o * LANES, LANES), LANES)],
            a_send.at[k], a_recv.at[o], o,
        ).wait_recv()

    quad = 4 * rows

    def rcopy(target):
        return remote(
            ret.at[pl.ds(pl.multiple_of(target * rows, rows), rows), :],
            out_ref.at[:, pl.ds(pl.multiple_of(me * cols, cols), cols)],
            r_send.at[target], r_recv.at[me], target,
        )

    own_ret = pltpu.make_async_copy(
        ret.at[pl.ds(pl.multiple_of(me * rows, rows), rows), :],
        out_ref.at[:, pl.ds(pl.multiple_of(me * cols, cols), cols)],
        ownret_sem,
    )

    @pl.loop(0, n)
    def _(s):
        down = acat[:, pl.ds(pl.multiple_of(s * LANES, LANES), LANES)]
        term = dot_f32(iall[s], down, NT).astype(BF16)
        back[:, pl.ds(pl.multiple_of(s * cap, cap), cap), :] = term.reshape(n, cap, cols)

    @pl.loop(0, nz)
    def _(i):
        zt = (z + 1 + i) % nz
        at = pl.ds(pl.multiple_of(zt * quad, quad), quad)
        base = dot_f32(gall[at, :], w_ref[...], NT)
        for t in range(4):
            d = zt * 4 + t
            pick = (
                lax.broadcasted_iota(jnp.int32, (n * cap, rows), 0) == pall[d, 1:2, :]
            ).astype(F32).astype(BF16)
            term = dot_f32(pick, back[d], TN)
            ret[pl.ds(pl.multiple_of(d * rows, rows), rows), :] = (
                base[t * rows:(t + 1) * rows] + term
            ).astype(BF16)
        for t in range(4):
            target = zt * 4 + t

            @pl.when(target != me)
            def _():
                rcopy(target).start()

            @pl.when(target == me)
            def _():
                own_ret.start()

    proj = jnp.zeros((n * cap, LANES), F32)
    for q in range(parts):
        own_x[q].wait()
        for k in range(1, n):
            o = (me + k) % n
            remote(
                xsel.at[q, pl.ds(0, cap), :],
                xrecv.at[q, pl.ds(pl.multiple_of(o * cap, cap), cap), :],
                x_send.at[q, k], x_recv.at[q, o], o,
            ).wait_recv()
        proj += jnp.dot(
            xrecv[q], a_ref[pl.ds(q * width, width), :], preferred_element_type=F32
        )

        @pl.loop(0, width // step)
        def _(i):
            at = pl.ds(pl.multiple_of(i * step, step), step)
            gin[q, at, :] = dot_f32(xrecv[q, :, at], ig[...], TN)

        pltpu.make_async_copy(
            gin.at[q], gin_ref.at[pl.ds(q * width, width), :], gin_sem.at[q]
        ).start()
    projected = (proj * keep).astype(BF16)
    gout[...] = scale * dot_f32(projected, rg[...], TN)
    out_copy = pltpu.make_async_copy(gout, gout_ref, gout_sem)
    out_copy.start()

    own_ret.wait()
    for k in range(1, n):
        o = (me + k) % n
        remote(
            ret.at[pl.ds(0, rows), :],
            out_ref.at[:, pl.ds(pl.multiple_of(o * cols, cols), cols)],
            r_send.at[o], r_recv.at[o], o,
        ).wait_recv()
        rcopy(o).wait_send()
        acopy(k).wait_send()
        pcopy(k).wait_send()
        for q in range(parts):
            xcopy(q, k).wait_send()
    g_drain()
    i_drain()
    for q in range(parts):
        pltpu.make_async_copy(
            gin.at[q], gin_ref.at[pl.ds(q * width, width), :], gin_sem.at[q]
        ).wait()
    out_copy.wait()


def routed(activations, out_grads, base_weight, adapter_in, adapter_out, tenant_ids, slot_of, ranks):
    n = lax.axis_size("ada")
    rows, dim = activations.shape
    dk = out_grads.shape[1]
    cap = max(2, 2 * rows // n)
    cols = dim // n
    parts = 8
    tenants = jnp.arange(slot_of.shape[0], dtype=jnp.int32)
    destination = jnp.sum(
        jnp.where(tenant_ids[:, None] == tenants[None, :], slot_of[None, :], 0), axis=1
    )
    earlier = jnp.arange(rows)[:, None] > jnp.arange(rows)[None, :]
    same = destination[:, None] == destination[None, :]
    position = jnp.sum((earlier & same).astype(jnp.int32), axis=1)
    placed = destination * cap + position
    place = jnp.zeros((8, rows), jnp.int32).at[0].set(destination).at[1].set(placed)
    slot_rank = jnp.sum(jnp.where(slot_of[None, :] == tenants[:, None], ranks[None, :], 0), axis=1)
    scale = 4.0 / jnp.sqrt(slot_rank.astype(F32))
    keep = (jnp.arange(LANES, dtype=jnp.int32)[None, :] < slot_rank[:, None]).astype(F32)
    mine = tenants == lax.axis_index("ada")
    own_scale = jnp.sum(jnp.where(mine, scale, 0.0))
    own_keep = jnp.sum(jnp.where(mine[:, None], keep, 0.0), axis=0)
    own = jnp.stack([own_scale * own_keep, own_keep, jnp.full((LANES,), own_scale)])
    own = jnp.pad(own, ((0, 5), (0, 0)))
    vmem = pl.BlockSpec(memory_space=pltpu.VMEM)
    any_space = pl.BlockSpec(memory_space=pl.ANY)
    dma = pltpu.SemaphoreType.DMA
    input_grads, grad_in, grad_out = pl.pallas_call(
        functools.partial(kernel, n, parts, 3),
        out_shape=(
            jax.ShapeDtypeStruct((rows, dim), BF16),
            jax.ShapeDtypeStruct((dim, LANES), F32),
            jax.ShapeDtypeStruct((LANES, dk), F32),
        ),
        in_specs=[vmem] * 7,
        out_specs=(any_space,) * 3,
        scratch_shapes=[
            pltpu.VMEM((n * rows, dk), BF16),
            pltpu.VMEM((n, n * cap, LANES), BF16),
            pltpu.VMEM((n, 8, rows), jnp.int32),
            pltpu.VMEM((cols, n * LANES), BF16),
            pltpu.VMEM((parts, n * cap, dim // parts), BF16),
            pltpu.VMEM((parts, n * cap, dim // parts), BF16),
            pltpu.VMEM((n * rows, cols), BF16),
            pltpu.VMEM((n, n * cap, cols), BF16),
            pltpu.VMEM((n * cap, LANES), BF16),
            pltpu.VMEM((n * cap, dk), BF16),
            pltpu.VMEM((parts, dim // parts, LANES), F32),
            pltpu.VMEM((LANES, dk), F32),
            dma((n,)), dma((4, n)),
            dma((n,)), dma((4, n)),
            dma((n,)), dma((n,)),
            dma((n,)), dma((n,)),
            dma((parts, n)), dma((parts, n)),
            dma((n,)), dma((n,)),
            dma((4 + parts,)), dma((parts,)), dma, dma,
        ],
        compiler_params=pltpu.CompilerParams(
            collective_id=0, has_side_effects=True, vmem_limit_bytes=56 * 2**20
        ),
        cost_estimate=pl.CostEstimate(
            flops=6 * 10**9, bytes_accessed=12 * 2**20, transcendentals=0
        ),
    )(activations, out_grads, adapter_out[0], base_weight, adapter_in[0], place, own)
    return (input_grads, grad_in[None], grad_out[None])


def base_term(out_grads, base_weight):
    return lax.dot_general(
        out_grads,
        lax.all_gather(base_weight, "ada", axis=0, tiled=True),
        (((1,), (1,)), ((), ())),
        preferred_element_type=jnp.float32,
    )


def adapter_part(activations, out_grads, adapter_in, adapter_out, tenant_ids, slot_of, ranks):
    peers = lax.axis_size("ada")
    local_rows = activations.shape[0]
    capacity = max(2, 2 * local_rows // peers)
    tenant_count = slot_of.shape[0]
    tenant_range = jnp.arange(tenant_count, dtype=jnp.int32)
    destination = jnp.sum(
        jnp.where(tenant_ids[:, None] == tenant_range[None, :], slot_of[None, :], 0), axis=1
    )
    onehot = (destination[:, None] == jnp.arange(peers, dtype=jnp.int32)[None, :]).astype(jnp.int32)
    running = jnp.cumsum(onehot, axis=0)
    position = jnp.sum(onehot * running, axis=1) - 1
    placed = destination * capacity + position
    selector = (placed[None, :] == jnp.arange(peers * capacity, dtype=jnp.int32)[:, None]).astype(
        jnp.bfloat16
    )
    send_x = jnp.dot(selector, activations, preferred_element_type=jnp.float32).astype(jnp.bfloat16)
    send_g = jnp.dot(selector, out_grads, preferred_element_type=jnp.float32).astype(jnp.bfloat16)
    recv_x, recv_g = (
        lax.all_to_all(send_x, "ada", split_axis=0, concat_axis=0, tiled=True),
        lax.all_to_all(send_g, "ada", split_axis=0, concat_axis=0, tiled=True),
    )
    owner_index = lax.axis_index("ada")
    own_rank = jnp.sum(jnp.where(slot_of == owner_index, ranks, 0))
    scale = 4.0 / jnp.sqrt(own_rank.astype(jnp.float32))
    keep = jnp.arange(adapter_in.shape[2], dtype=jnp.int32) < own_rank
    down = jnp.where(keep[None, :], adapter_in[0], jnp.zeros_like(adapter_in[0]))
    upper = jnp.where(keep[:, None], adapter_out[0], jnp.zeros_like(adapter_out[0]))
    projected = jnp.dot(recv_x, down, preferred_element_type=jnp.float32).astype(jnp.bfloat16)
    inner_grad = (
        scale
        * lax.dot_general(
            recv_g, upper, (((1,), (1,)), ((), ())), preferred_element_type=jnp.float32
        )
    ).astype(jnp.bfloat16)
    grad_out = scale * lax.dot_general(
        projected, recv_g, (((0,), (0,)), ((), ())), preferred_element_type=jnp.float32
    )
    grad_in = lax.dot_general(
        recv_x, inner_grad, (((0,), (0,)), ((), ())), preferred_element_type=jnp.float32
    )
    returned = lax.dot_general(
        inner_grad, down, (((1,), (1,)), ((), ())), preferred_element_type=jnp.float32
    ).astype(jnp.bfloat16)
    arrived = lax.all_to_all(returned, "ada", split_axis=0, concat_axis=0, tiled=True)
    adapter_term = lax.dot_general(
        selector, arrived, (((0,), (0,)), ((), ())), preferred_element_type=jnp.float32
    )
    return (adapter_term, grad_in[None], grad_out[None])


def gathered(
    activations, out_grads, base_weight, adapter_in, adapter_out, tenant_ids, slot_of, ranks
):
    base = base_term(out_grads, base_weight)
    adapter_term, grad_in, grad_out = adapter_part(
        activations, out_grads, adapter_in, adapter_out, tenant_ids, slot_of, ranks
    )
    input_grads = (base + adapter_term).astype(jnp.bfloat16)
    return (input_grads, grad_in, grad_out)


def shards(activations, *rest):
    n = lax.axis_size("ada")
    rows, dim = activations.shape
    whole = n % 4 == 0 and rows == LANES and (2 * rows // n) % 16 == 0 and dim % (512 * n) == 0 and n >= 8
    return (routed if whole else gathered)(activations, *rest)


def solution(mesh):
    placed = (
        P(("rep", "ada"), None),
        P(("rep", "ada"), None),
        P("ada", None),
        P(("rep", "ada"), None, None),
        P(("rep", "ada"), None, None),
        P(("rep", "ada")),
        P("rep"),
        P("rep"),
    )
    return jax.shard_map(
        shards,
        mesh=mesh,
        in_specs=placed,
        out_specs=(
            P(("rep", "ada"), None),
            P(("rep", "ada"), None, None),
            P(("rep", "ada"), None, None),
        ),
        check_vma=False,
    )
```
